128 devices in a mesh: chan: 16 (over y, z_lo, core), sub: 8 (over x, z_hi).
Axes of the slice: x: 4, y: 4, z: 4 (z_hi: 2, z_lo: 2; z = z_hi * 2 + z_lo), core: 2. Of those that a mesh axis runs over, the one named last changes fastest.
Arguments:
- spectra: bfloat16 [8, 2, 512, 32768], P('sub', None, None, 'chan'), may hold values from -12 to 12
- filter_init: float32 [2, 32768], P(None, 'chan'), may hold values from -2.1 to 2.1
- profile_init: float32 [2, 512], replicated, may hold values from -1.4 to 1.4
Outputs:
- filter_out: float32 [2, 32768], P(None, 'chan')
- profile_out: float32 [2, 512], replicated
- misfit: float32 [1], replicated
The draws below stay inside these ranges and needn't reach their ends.
All inputs are finite; a program needn't handle non-finite values.
Results may differ from the reference program's by a relative error of at most 0.0003.
Values sent between devices are 32-bit elements; how exact they have to be, the bound alone decides.
No kernel may reach another device: no remote copies, remote signals or barrier semaphores. Data moves between devices by JAX's collectives and lax.ppermute only.
A program may use at most 128 MiB of HBM per device.

```python
import jax
import jax.numpy as jnp
from jax import lax

CHANNELS = 32768
HARM = 512
ITERS = 1
SUBS = 8


def draw_start(key):
    subkeys = jax.random.split(jax.random.fold_in(key, 5), 2)
    filt = jnp.clip(0.7 * jax.random.normal(subkeys[0], (2, CHANNELS), jnp.float32), -2.1, 2.1)
    prof = jnp.clip(0.7 * jax.random.normal(subkeys[1], (2, HARM), jnp.float32), -1.4, 1.4)
    return (filt, prof)


def draw_filter_init(key, part):
    return draw_start(key)[0].astype(jnp.float32)


def draw_profile_init(key, part):
    return draw_start(key)[1].astype(jnp.float32)


def start_model(filt, prof):
    padded = jnp.pad(filt, ((0, 0), (HARM, HARM)))

    def one_row(harmonic):
        forward = lax.dynamic_slice_in_dim(padded, HARM + harmonic, CHANNELS, 1)
        backward = lax.dynamic_slice_in_dim(padded, HARM - harmonic, CHANNELS, 1)
        prod_re = forward[0] * backward[0] + forward[1] * backward[1]
        prod_im = forward[1] * backward[0] - forward[0] * backward[1]
        prof_re = prof[0, harmonic]
        prof_im = prof[1, harmonic]
        return jnp.stack([prod_re * prof_re - prod_im * prof_im, prod_re * prof_im + prod_im * prof_re])
    rows = jax.vmap(one_row)(jnp.arange(HARM).astype(jnp.int32))
    return jnp.transpose(rows, (1, 0, 2))


def draw_spectra(key, part):
    filt, prof = draw_start(key)
    model = start_model(filt, prof)
    subkeys = jax.random.split(jax.random.fold_in(key, 11), 1)
    channel_pos = jnp.arange(CHANNELS).astype(jnp.float32) / CHANNELS
    sub_pos = jnp.arange(SUBS).astype(jnp.float32) / SUBS
    levels = (0.4 + 0.8 * channel_pos)[None, None, None, :] * (0.7 + 0.6 * sub_pos)[:, None, None, None]
    noise = jax.random.normal(subkeys[0], (SUBS, 2, HARM, CHANNELS), jnp.float32) * levels
    values = model[None] + 0.5 * noise
    return jnp.clip(values, -12.0, 12.0).astype(jnp.bfloat16)


def setup_inputs(seed: int = 0) -> dict:
    arg_keys = jax.random.split(jax.random.key(seed), 4)
    return {
        "spectra": draw_spectra(jax.random.fold_in(arg_keys[3], 71), 0),
        "filter_init": draw_filter_init(jax.random.fold_in(arg_keys[3], 71), 0),
        "profile_init": draw_profile_init(jax.random.fold_in(arg_keys[3], 71), 0),
    }


filter_rate = 0.1
profile_rate = 0.1
epsilon = 1e-06

def energy(filt, prof, spectrum):
    padded = jnp.pad(filt, ((0, 0), (HARM, HARM)))
    channel_idx = jnp.arange(CHANNELS).astype(jnp.int32)[None, :]
    harmonic_idx = jnp.arange(HARM).astype(jnp.int32)[:, None]
    forward = padded[:, HARM + channel_idx + harmonic_idx]
    backward = padded[:, HARM + channel_idx - harmonic_idx]
    prod_re = forward[0] * backward[0] + forward[1] * backward[1]
    prod_im = forward[1] * backward[0] - forward[0] * backward[1]
    prof_re = prof[0][:, None]
    prof_im = prof[1][:, None]
    model_re = prod_re * prof_re - prod_im * prof_im
    model_im = prod_re * prof_im + prod_im * prof_re
    resid_re = spectrum[0] - model_re
    resid_im = spectrum[1] - model_im
    return jnp.sum(resid_re * resid_re + resid_im * resid_im)

def reference(spectra, filter_init, profile_init):
    norm_scale = 1.0 / (SUBS * HARM)
    filt = filter_init
    prof = profile_init
    misfits = []
    for iteration in range(ITERS):

        def accumulate(totals, spectrum):
            energy_value, grads = jax.value_and_grad(energy, argnums=(0, 1))(filt, prof, spectrum.astype(jnp.float32))
            return ((totals[0] + energy_value, totals[1] + grads[0], totals[2] + grads[1]), None)
        start_sums = (jnp.zeros((), jnp.float32), jnp.zeros_like(filt), jnp.zeros_like(prof))
        totals, unused = lax.scan(accumulate, start_sums, spectra)
        error = totals[0] * norm_scale
        filter_grad = totals[1] * norm_scale
        profile_grad = totals[2] * norm_scale
        misfits.append(error / CHANNELS)
        filt = filt - filter_rate * filter_grad / jnp.sqrt(jnp.sum(filter_grad * filter_grad) / (2 * CHANNELS) + epsilon)
        prof = prof - profile_rate * profile_grad / jnp.sqrt(jnp.mean(profile_grad * profile_grad) + epsilon)
    return (filt, prof, jnp.stack(misfits))
```

```python
import functools

import jax
import jax.numpy as jnp
from jax import lax
from jax.experimental import pallas as pl
from jax.experimental.pallas import tpu as pltpu
from jax.sharding import PartitionSpec as P

CHANNELS = 32768
LANES = 128
ROWS = 128
GROUP = 16

filter_rate = 0.1
profile_rate = 0.1
epsilon = 1e-06


def skew(block, sign):
    width = block.shape[1]
    row = lax.broadcasted_iota(jnp.int32, block.shape, 0)
    for bit in (1, 2, 4):
        moved = pltpu.roll(block, bit if sign > 0 else width - bit, 1)
        block = jnp.where((row & bit) != 0, moved, block)
    return block


def gradient_kernel(
    factor, spectra, low, own, high, prof, out,
    fwd_re, fwd_im, bwd_re, bwd_im, up_re, up_im, down_re, down_im, part_re, part_im, err
):
    step = pl.program_id(0)
    owned = own.shape[1]
    halo = low.shape[1]
    width = owned + 2 * halo
    harmonics = prof.shape[0]
    chan = lax.axis_index("chan")
    last = lax.axis_size("chan") - 1

    @pl.when(step == 0)
    def _():
        keep_low = jnp.where(chan == 0, 0.0, 1.0).astype(jnp.float32)
        keep_high = jnp.where(chan == last, 0.0, 1.0).astype(jnp.float32)
        for part, fwd, bwd in ((0, fwd_re, bwd_re), (1, fwd_im, bwd_im)):
            line = jnp.concatenate(
                [
                    low[part : part + 1, :] * keep_low,
                    own[part : part + 1, :],
                    high[part : part + 1, :] * keep_high,
                ],
                axis=1,
            )
            base = jnp.broadcast_to(line, (8, width))
            right = skew(base, 1)
            left = skew(base, -1)
            for a in range(ROWS // 8):
                rows = pl.ds(8 * a, 8)
                bwd[rows, :] = pltpu.roll(right, 8 * a, 1) if a else right
                fwd[rows, :] = pltpu.roll(left, width - 8 * a, 1) if a else left
        for acc in (up_re, up_im, down_re, down_im):
            acc[...] = jnp.zeros_like(acc)
        err[...] = jnp.zeros_like(err)

    shift = step * ROWS

    def group(index, carry):
        start = pl.multiple_of(index * GROUP, GROUP)
        rows = pl.ds(start, GROUP)
        krows = pl.ds(pl.multiple_of(shift + start, GROUP), GROUP)
        q_re = jnp.broadcast_to(prof[krows, 0:1], (GROUP, LANES))
        q_im = jnp.broadcast_to(prof[krows, 1:2], (GROUP, LANES))
        a_re = jnp.zeros((GROUP, LANES), jnp.float32)
        a_im = jnp.zeros((GROUP, LANES), jnp.float32)
        e_sum = jnp.zeros((GROUP, LANES), jnp.float32)
        for tile in range(owned // LANES):
            cols = pl.ds(tile * LANES, LANES)
            above = pl.ds(pl.multiple_of(halo + tile * LANES + shift, LANES), LANES)
            below = pl.ds(pl.multiple_of(halo + tile * LANES - shift, LANES), LANES)
            s_re = spectra[0, 0, rows, cols].astype(jnp.float32)
            s_im = spectra[0, 1, rows, cols].astype(jnp.float32)
            f_re = fwd_re[rows, above]
            f_im = fwd_im[rows, above]
            b_re = bwd_re[rows, below]
            b_im = bwd_im[rows, below]
            p_re = f_re * b_re + f_im * b_im
            p_im = f_im * b_re - f_re * b_im
            r_re = s_re - (p_re * q_re - p_im * q_im)
            r_im = s_im - (p_re * q_im + p_im * q_re)
            e_sum = e_sum + (r_re * r_re + r_im * r_im)
            a_re = a_re + (r_re * p_re + r_im * p_im)
            a_im = a_im + (r_im * p_re - r_re * p_im)
            x_re = r_re * q_re + r_im * q_im
            x_im = r_im * q_re - r_re * q_im
            up_re[rows, above] += x_re * b_re - x_im * b_im
            up_im[rows, above] += x_re * b_im + x_im * b_re
            down_re[rows, below] += x_re * f_re + x_im * f_im
            down_im[rows, below] += x_re * f_im - x_im * f_re
        part_re[krows, :] = a_re
        part_im[krows, :] = a_im
        err[...] += e_sum
        return carry

    lax.fori_loop(0, ROWS // GROUP, group, 0)

    @pl.when(step == pl.num_programs(0) - 1)
    def _():
        ones = jnp.ones((8, LANES), jnp.float32)
        for part, up, down, sums in (
            (0, up_re, down_re, part_re),
            (1, up_im, down_im, part_im),
        ):
            total_up = up[0:8, :]
            total_down = down[0:8, :]
            for a in range(1, ROWS // 8):
                rows = pl.ds(8 * a, 8)
                total_up = total_up + pltpu.roll(up[rows, :], 8 * a, 1)
                total_down = total_down + pltpu.roll(down[rows, :], width - 8 * a, 1)
            total = skew(total_up, 1) + skew(total_down, -1)
            line = factor * jnp.sum(total, axis=0, keepdims=True)
            out[part : part + 1, 0:width] = line
            reduced = lax.dot_general(
                ones,
                sums[...],
                (((1,), (1,)), ((), ())),
                precision=lax.Precision.HIGHEST,
                preferred_element_type=jnp.float32,
            )
            out[part : part + 1, width : width + harmonics] = factor * reduced[0:1, :]
        out[0:1, width + harmonics :] = jnp.sum(err[...], axis=0, keepdims=True)
        out[1:2, width + harmonics :] = jnp.zeros((1, LANES), jnp.float32)


def local_gradients(factor, spectra, low, own, high, prof):
    harmonics = prof.shape[0]
    halo = low.shape[1]
    owned = own.shape[1]
    width = owned + 2 * halo
    table = pltpu.VMEM((ROWS, width), jnp.float32)
    whole = lambda shape: pl.BlockSpec(shape, lambda i: (0, 0))
    return pl.pallas_call(
        functools.partial(gradient_kernel, factor),
        grid=(harmonics // ROWS,),
        in_specs=[
            pl.BlockSpec((1, 2, ROWS, owned), lambda i: (0, 0, i, 0)),
            whole(low.shape),
            whole(own.shape),
            whole(high.shape),
            whole(prof.shape),
        ],
        out_specs=whole((2, width + harmonics + LANES)),
        out_shape=jax.ShapeDtypeStruct((2, width + harmonics + LANES), jnp.float32),
        scratch_shapes=[table] * 8
        + [pltpu.VMEM((harmonics, LANES), jnp.float32)] * 2
        + [pltpu.VMEM((GROUP, LANES), jnp.float32)],
        compiler_params=pltpu.CompilerParams(vmem_limit_bytes=40 * 1024 * 1024),
    )(spectra, low, own, high, prof)


def neighbours(to_next, to_previous, axis):
    count = lax.axis_size(axis)
    ahead = [(i, (i + 1) % count) for i in range(count)]
    back = [(target, source) for source, target in ahead]
    return lax.ppermute(to_next, axis, ahead), lax.ppermute(to_previous, axis, back)


def sum_over(values, axis, masks):
    count = lax.axis_size(axis)
    for mask in masks:
        values = values + lax.ppermute(values, axis, [(i, i ^ mask) for i in range(count)])
    return values


def on_device(spectra, filter_init, profile_init):
    harmonics = profile_init.shape[1]
    owned = filter_init.shape[1]
    weight = 1.0 / (lax.axis_size("sub") * spectra.shape[0] * harmonics)
    chan = lax.axis_index("chan")
    low, high = neighbours(filter_init[:, owned - harmonics :], filter_init[:, :harmonics], "chan")
    sums = local_gradients(-2.0 * weight, spectra, low, filter_init, high, profile_init.T)
    from_below, from_above = neighbours(
        sums[:, harmonics + owned : 2 * harmonics + owned], sums[:, :harmonics], "chan"
    )
    from_below = jnp.where(chan == 0, 0.0, from_below)
    from_above = jnp.where(chan == lax.axis_size("chan") - 1, 0.0, from_above)
    local = sums[:, harmonics : harmonics + owned]
    local = jnp.concatenate(
        [
            local[:, :harmonics] + from_below,
            local[:, harmonics : owned - harmonics],
            local[:, owned - harmonics :] + from_above,
            sums[:, owned + 2 * harmonics :],
        ],
        axis=1,
    )
    local = sum_over(local, "sub", (2, 6, 1))
    filter_grad = local[:, :owned]
    squares = jnp.sum(filter_grad * filter_grad)
    rest = local[:, owned:]
    rest = rest.at[1, harmonics].set(squares)
    rest = sum_over(rest, "chan", (1, 2, 4, 12))
    profile_grad = rest[:, :harmonics]
    error_total = jnp.sum(rest[0, harmonics:])
    squares = rest[1, harmonics]
    filter_out = filter_init - filter_rate * filter_grad / jnp.sqrt(
        squares / (2 * CHANNELS) + epsilon
    )
    profile_out = profile_init - profile_rate * profile_grad / jnp.sqrt(
        jnp.mean(profile_grad * profile_grad) + epsilon
    )
    return (filter_out, profile_out, (error_total * weight / CHANNELS)[None])


def solution(mesh):
    return jax.shard_map(
        on_device,
        mesh=mesh,
        in_specs=(P("sub", None, None, "chan"), P(None, "chan"), P()),
        out_specs=(P(None, "chan"), P(), P()),
        check_vma=False,
    )
```

```python
import functools

import jax
import jax.numpy as jnp
from jax import lax
from jax.experimental import pallas as pl
from jax.experimental.pallas import tpu as pltpu
from jax.sharding import PartitionSpec as P

CHANNELS = 32768
LANES = 128
ROWS = 128
GROUP = 16
UNROLL = 2
VMEM_LIMIT = 24 * 1024 * 1024

filter_rate = 0.1
profile_rate = 0.1
epsilon = 1e-06


def skew(block, sign):
    width = block.shape[1]
    row = lax.broadcasted_iota(jnp.int32, block.shape, 0)
    for bit in (1, 2, 4):
        moved = pltpu.roll(block, bit if sign > 0 else width - bit, 1)
        block = jnp.where((row & bit) != 0, moved, block)
    return block


def gradient_kernel(
    factor, spectra, own_hbm, prof_hbm, prev, after, out,
    data, own, prof, fwd_re, fwd_im, bwd_re, bwd_im, up_re, up_im, down_re, down_im,
    q_re, q_im, part_re, part_im, err, block_sems, sems,
):
    owned = own.shape[1]
    harmonics = prof.shape[1]
    halo = harmonics
    width = owned + 2 * halo
    blocks = harmonics // ROWS
    edge = halo // LANES
    tiles = owned // LANES
    chan = lax.axis_index("chan")
    last = lax.axis_size("chan") - 1
    copies = [
        pltpu.make_async_copy(
            spectra.at[0, :, pl.ds(q * ROWS, ROWS), :],
            data.at[:, pl.ds(q * ROWS, ROWS), :],
            block_sems.at[q],
        )
        for q in range(blocks)
    ]
    own_copy = pltpu.make_async_copy(own_hbm, own, sems.at[0])
    prof_copy = pltpu.make_async_copy(prof_hbm, prof, sems.at[1])
    own_copy.start()
    prof_copy.start()
    for copy in copies:
        copy.start()

    for acc in (up_re, up_im):
        acc[:, halo - LANES : halo] = jnp.zeros((ROWS, LANES), jnp.float32)
        acc[:, halo + owned :] = jnp.zeros((ROWS, halo), jnp.float32)
    for acc in (down_re, down_im):
        acc[:, :halo] = jnp.zeros((ROWS, halo), jnp.float32)
        acc[:, halo + owned : halo + owned + LANES] = jnp.zeros((ROWS, LANES), jnp.float32)

    keep_low = jnp.where(chan == 0, 0.0, 1.0).astype(jnp.float32)
    keep_high = jnp.where(chan == last, 0.0, 1.0).astype(jnp.float32)
    own_copy.wait()
    reach = halo - ROWS
    for part, fwd, bwd in ((0, fwd_re, bwd_re), (1, fwd_im, bwd_im)):
        line = jnp.concatenate(
            [
                prev[part : part + 1, owned - halo :] * keep_low,
                own[part : part + 1, :],
                after[part : part + 1, :halo] * keep_high,
            ],
            axis=1,
        )
        base = jnp.broadcast_to(line, (8, width))
        right = skew(base, 1)
        left = skew(base, -1)
        for a in range(ROWS // 8):
            rows = pl.ds(8 * a, 8)
            moved = pltpu.roll(right, 8 * a, 1) if a else right
            bwd[rows, halo - reach : halo + owned] = moved[:, halo - reach : halo + owned]
            moved = pltpu.roll(left, width - 8 * a, 1) if a else left
            fwd[rows, halo : halo + owned + reach] = moved[:, halo : halo + owned + reach]

    prof_copy.wait()
    columns = jnp.transpose(
        jnp.concatenate([prof[...], jnp.zeros((6, harmonics), jnp.float32)], axis=0)
    )
    q_re[...] = jnp.broadcast_to(columns[:, 0:1], (harmonics, LANES))
    q_im[...] = jnp.broadcast_to(columns[:, 1:2], (harmonics, LANES))
    err[...] = jnp.zeros_like(err)

    for q in range(blocks):
        copies[q].wait()

        def group(index, carry, q=q):
            start = pl.multiple_of(index * GROUP, GROUP)
            rows = pl.ds(start, GROUP)
            krows = pl.ds(pl.multiple_of(q * ROWS + start, GROUP), GROUP)
            w_re = q_re[krows, :]
            w_im = q_im[krows, :]
            a_re = jnp.zeros((GROUP, LANES), jnp.float32)
            a_im = jnp.zeros((GROUP, LANES), jnp.float32)
            e_sum = jnp.zeros((GROUP, LANES), jnp.float32)
            for tile in range(tiles):
                cols = pl.ds(tile * LANES, LANES)
                above = pl.ds((edge + tile + q) * LANES, LANES)
                below = pl.ds((edge + tile - q) * LANES, LANES)
                s_re = data[0, krows, cols].astype(jnp.float32)
                s_im = data[1, krows, cols].astype(jnp.float32)
                f_re = fwd_re[rows, above]
                f_im = fwd_im[rows, above]
                b_re = bwd_re[rows, below]
                b_im = bwd_im[rows, below]
                p_re = f_re * b_re + f_im * b_im
                p_im = f_im * b_re - f_re * b_im
                r_re = s_re - (p_re * w_re - p_im * w_im)
                r_im = s_im - (p_re * w_im + p_im * w_re)
                e_sum = e_sum + (r_re * r_re + r_im * r_im)
                a_re = a_re + (r_re * p_re + r_im * p_im)
                a_im = a_im + (r_im * p_re - r_re * p_im)
                x_re = r_re * w_re + r_im * w_im
                x_im = r_im * w_re - r_re * w_im
                u_re = x_re * b_re - x_im * b_im
                u_im = x_re * b_im + x_im * b_re
                d_re = x_re * f_re + x_im * f_im
                d_im = x_re * f_im - x_im * f_re
                if q == 0:
                    up_re[rows, above] = u_re
                    up_im[rows, above] = u_im
                    down_re[rows, below] = d_re
                    down_im[rows, below] = d_im
                else:
                    up_re[rows, above] += u_re
                    up_im[rows, above] += u_im
                    down_re[rows, below] += d_re
                    down_im[rows, below] += d_im
            part_re[krows, :] = a_re
            part_im[krows, :] = a_im
            err[...] += e_sum
            return carry

        lax.fori_loop(0, ROWS // GROUP, group, 0, unroll=UNROLL)

    ones = jnp.ones((8, LANES), jnp.float32)
    span = (owned + halo) // 2
    for part, up, down, sums in (
        (0, up_re, down_re, part_re),
        (1, up_im, down_im, part_im),
    ):
        raised = []
        lowered = []
        for half in range(2):
            first = halo - LANES + half * span
            total = up[0:8, first : first + span + LANES]
            for a in range(1, ROWS // 8):
                piece = up[8 * a : 8 * a + 8, first : first + span + LANES]
                total = total + pltpu.roll(piece, 8 * a, 1)
            raised.append(jnp.sum(skew(total, 1)[:, LANES:], axis=0, keepdims=True))
            first = half * span
            total = down[0:8, first : first + span + LANES]
            for a in range(1, ROWS // 8):
                piece = down[8 * a : 8 * a + 8, first : first + span + LANES]
                total = total + pltpu.roll(piece, span + LANES - 8 * a, 1)
            lowered.append(jnp.sum(skew(total, -1)[:, :span], axis=0, keepdims=True))
        raised = jnp.concatenate(raised, axis=1) * factor
        lowered = jnp.concatenate(lowered, axis=1) * factor
        row = slice(part, part + 1)
        out[row, 0:halo] = lowered[:, :halo] * keep_low
        out[row, halo : halo + owned] = lowered[:, halo:] + raised[:, :owned]
        out[row, halo + owned : width] = raised[:, owned:] * keep_high
        reduced = lax.dot_general(
            ones,
            sums[...],
            (((1,), (1,)), ((), ())),
            precision=lax.Precision.HIGHEST,
            preferred_element_type=jnp.float32,
        )
        out[row, width : width + harmonics] = factor * reduced[0:1, :]
    out[0:1, width + harmonics :] = jnp.sum(err[...], axis=0, keepdims=True)
    out[1:2, width + harmonics :] = jnp.zeros((1, LANES), jnp.float32)


def local_gradients(factor, spectra, own, prof, prev, after):
    harmonics = prof.shape[1]
    owned = own.shape[1]
    width = owned + 2 * harmonics
    table = pltpu.VMEM((ROWS, width), jnp.float32)
    column = pltpu.VMEM((harmonics, LANES), jnp.float32)
    anywhere = pl.BlockSpec(memory_space=pltpu.HBM)
    inside = pl.BlockSpec(memory_space=pltpu.VMEM)
    return pl.pallas_call(
        functools.partial(gradient_kernel, factor),
        in_specs=[anywhere, anywhere, anywhere, inside, inside],
        out_specs=inside,
        out_shape=jax.ShapeDtypeStruct((2, width + harmonics + LANES), jnp.float32),
        scratch_shapes=[
            pltpu.VMEM((2, harmonics, owned), jnp.bfloat16),
            pltpu.VMEM((2, owned), jnp.float32),
            pltpu.VMEM((2, harmonics), jnp.float32),
        ]
        + [table] * 8
        + [column] * 4
        + [
            pltpu.VMEM((GROUP, LANES), jnp.float32),
            pltpu.SemaphoreType.DMA((harmonics // ROWS,)),
            pltpu.SemaphoreType.DMA((2,)),
        ],
        compiler_params=pltpu.CompilerParams(vmem_limit_bytes=VMEM_LIMIT),
    )(*(pltpu.with_memory_space_constraint(x, pltpu.HBM) for x in (spectra, own, prof)), prev, after)


def final_kernel(weight, sums, grads, low_add, high_add, filt, prof, filt_out, prof_out, misfit):
    harmonics = prof.shape[1]
    owned = filt.shape[1]
    halo = harmonics
    squares = jnp.sum(sums[:, harmonics + LANES :])
    scale = filter_rate / jnp.sqrt(jnp.full((2, LANES), squares) / (2 * CHANNELS) + epsilon)
    scale = scale[:, 0:1]
    low = grads[:, halo : 2 * halo] + low_add[:, halo:]
    middle = grads[:, 2 * halo : owned]
    high = grads[:, owned : owned + halo] + high_add[:, :halo]
    filt_out[:, :halo] = filt[:, :halo] - scale * low
    filt_out[:, halo : owned - halo] = filt[:, halo : owned - halo] - scale * middle
    filt_out[:, owned - halo :] = filt[:, owned - halo :] - scale * high
    grad = sums[:, :harmonics]
    mean = jnp.sum(grad * grad) / (2 * harmonics)
    rate = profile_rate / jnp.sqrt(jnp.full((2, LANES), mean) + epsilon)
    prof_out[...] = prof[...] - rate[:, 0:1] * grad
    total = jnp.sum(sums[:, harmonics : harmonics + LANES])
    misfit[0] = total * (weight / CHANNELS)


def update(weight, sums, grads, low_add, high_add, filt, prof):
    inside = pl.BlockSpec(memory_space=pltpu.VMEM)
    return pl.pallas_call(
        functools.partial(final_kernel, weight),
        in_specs=[inside] * 6,
        out_specs=[inside, inside, pl.BlockSpec(memory_space=pltpu.SMEM)],
        out_shape=[
            jax.ShapeDtypeStruct(filt.shape, jnp.float32),
            jax.ShapeDtypeStruct(prof.shape, jnp.float32),
            jax.ShapeDtypeStruct((1,), jnp.float32),
        ],
        compiler_params=pltpu.CompilerParams(vmem_limit_bytes=2 * 1024 * 1024),
    )(sums, grads, low_add, high_add, filt, prof)


def fold(values):
    total = values[:, :LANES]
    for start in range(LANES, values.shape[1], LANES):
        total = total + values[:, start : start + LANES]
    return total


def swap(values, axis, mask):
    count = lax.axis_size(axis)
    return lax.ppermute(values, axis, [(i, i ^ mask) for i in range(count)])


def neighbours(to_next, to_previous, axis):
    count = lax.axis_size(axis)
    ahead = [(i, (i + 1) % count) for i in range(count)]
    back = [(target, source) for source, target in ahead]
    return lax.ppermute(to_next, axis, ahead), lax.ppermute(to_previous, axis, back)


def join_blocks(sums, low_edge, high_edge, axis, masks):
    chan = lax.axis_index(axis)
    size = sums.shape[1]
    span = low_edge.shape[1]
    low_add = jnp.zeros_like(low_edge)
    high_add = jnp.zeros_like(high_edge)
    for step, mask in enumerate(masks):
        is_low = (chan >> step) & 1 == 0
        place = chan & ((1 << step) - 1)
        if step < len(masks) - 1:
            got = swap(jnp.concatenate([sums, low_edge, high_edge], axis=1), axis, mask)
            facing = jnp.where(is_low, got[:, size : size + span], got[:, size + span :])
        else:
            got = swap(jnp.concatenate([sums, jnp.where(is_low, high_edge, low_edge)], axis=1), axis, mask)
            facing = got[:, size:]
        mine = jnp.where(is_low, high_edge, low_edge)
        cross = 2.0 * fold(mine * facing)
        sums = sums + got[:, :size]
        sums = jnp.concatenate([sums[:, : size - LANES], sums[:, size - LANES :] + cross], axis=1)
        high_add = jnp.where(is_low & (place == (1 << step) - 1), facing, high_add)
        low_add = jnp.where(~is_low & (place == 0), facing, low_add)
        if step < len(masks) - 1:
            low_edge = jnp.where(is_low, low_edge, got[:, size : size + span])
            high_edge = jnp.where(is_low, got[:, size + span :], high_edge)
    return sums, low_add, high_add


def on_device(spectra, filter_init, profile_init):
    harmonics = profile_init.shape[1]
    owned = filter_init.shape[1]
    width = owned + 2 * harmonics
    weight = 1.0 / (lax.axis_size("sub") * spectra.shape[0] * harmonics)
    prev, after = neighbours(filter_init, filter_init, "chan")
    local = local_gradients(-2.0 * weight, spectra, filter_init, profile_init, prev, after)
    for mask in (2, 6, 1):
        local = local + swap(local, "sub", mask)
    grads = local[:, :width]
    sums = jnp.concatenate([local[:, width:], fold(grads * grads)], axis=1)
    sums, low_add, high_add = join_blocks(
        sums, grads[:, : 2 * harmonics], grads[:, owned:], "chan", (1, 2, 4, 12)
    )
    return tuple(update(weight, sums, grads, low_add, high_add, filter_init, profile_init))


def solution(mesh):
    return jax.shard_map(
        on_device,
        mesh=mesh,
        in_specs=(P("sub", None, None, "chan"), P(None, "chan"), P()),
        out_specs=(P(None, "chan"), P(), P()),
        check_vma=False,
    )
```

```python
import functools

import jax
import jax.numpy as jnp
from jax import lax
from jax.experimental import pallas as pl
from jax.experimental.pallas import tpu as pltpu
from jax.sharding import PartitionSpec as P

CHANNELS = 32768
LANES = 128
ROWS = 128
GROUP = 16
UNROLL = 2
VMEM_LIMIT = 28 * 1024 * 1024

filter_rate = 0.1
profile_rate = 0.1
epsilon = 1e-06


def skew(block, sign):
    width = block.shape[1]
    row = lax.broadcasted_iota(jnp.int32, block.shape, 0)
    for bit in (1, 2, 4):
        moved = pltpu.roll(block, bit if sign > 0 else width - bit, 1)
        block = jnp.where((row & bit) != 0, moved, block)
    return block


def gradient_kernel(
    factor, spectra, prof_hbm, own, prev, after, out,
    data, prof, fwd_re, fwd_im, fwd_sum, fwd_dif, bwd_re, bwd_sum, bwd_dif,
    up_re, up_im, down_re, down_im,
    unit_re, unit_im, size, part_re, part_im, err, block_sems, prof_sem,
):
    owned = own.shape[1]
    harmonics = prof.shape[1]
    halo = harmonics
    width = owned + 2 * halo
    blocks = harmonics // ROWS
    edge = halo // LANES
    tiles = owned // LANES
    chan = lax.axis_index("chan")
    last = lax.axis_size("chan") - 1
    copies = [
        pltpu.make_async_copy(
            spectra.at[0, :, pl.ds(q * ROWS, ROWS), :],
            data.at[:, pl.ds(q * ROWS, ROWS), :],
            block_sems.at[q],
        )
        for q in range(blocks)
    ]
    prof_copy = pltpu.make_async_copy(prof_hbm, prof, prof_sem)
    prof_copy.start()
    for copy in copies:
        copy.start()

    for acc in (up_re, up_im):
        acc[:, halo - LANES : halo] = jnp.zeros((ROWS, LANES), jnp.float32)
        acc[:, halo + owned :] = jnp.zeros((ROWS, halo), jnp.float32)
    for acc in (down_re, down_im):
        acc[:, :halo] = jnp.zeros((ROWS, halo), jnp.float32)
        acc[:, halo + owned : halo + owned + LANES] = jnp.zeros((ROWS, LANES), jnp.float32)

    keep_low = jnp.where(chan == 0, 0.0, 1.0).astype(jnp.float32)
    keep_high = jnp.where(chan == last, 0.0, 1.0).astype(jnp.float32)
    reach = halo - ROWS
    lines = [
        jnp.concatenate(
            [
                prev[part : part + 1, owned - halo :] * keep_low,
                own[part : part + 1, :],
                after[part : part + 1, :halo] * keep_high,
            ],
            axis=1,
        )
        for part in range(2)
    ]
    bases = [jnp.broadcast_to(line, (8, width)) for line in lines]
    rights = [skew(base, 1) for base in bases]
    lefts = [skew(base, -1) for base in bases]
    behind = slice(halo - reach, halo + owned)
    ahead = slice(halo, halo + owned + reach)
    for a in range(ROWS // 8):
        rows = pl.ds(8 * a, 8)
        re, im = ((pltpu.roll(x, 8 * a, 1) if a else x)[:, behind] for x in rights)
        bwd_re[rows, behind] = re
        bwd_sum[rows, behind] = re + im
        bwd_dif[rows, behind] = re - im
        re, im = ((pltpu.roll(x, width - 8 * a, 1) if a else x)[:, ahead] for x in lefts)
        fwd_re[rows, ahead] = re
        fwd_im[rows, ahead] = im
        fwd_sum[rows, ahead] = re + im
        fwd_dif[rows, ahead] = re - im

    prof_copy.wait()
    prof_re = prof[0:1, :]
    prof_im = prof[1:2, :]
    length = jnp.sqrt(prof_re * prof_re + prof_im * prof_im)
    present = length > 0.0
    divisor = jnp.where(present, length, 1.0)
    turn_re = jnp.where(present, prof_re / divisor, 1.0)
    turn_im = jnp.where(present, prof_im / divisor, 0.0)
    columns = jnp.transpose(
        jnp.concatenate([turn_re, turn_im, length, jnp.zeros((5, harmonics), jnp.float32)], axis=0)
    )
    for index, table in enumerate((unit_re, unit_im, size)):
        table[...] = jnp.broadcast_to(columns[:, index : index + 1], (harmonics, LANES))
    err[...] = jnp.zeros_like(err)

    for q in range(blocks):
        copies[q].wait()

        def group(index, carry, q=q):
            start = pl.multiple_of(index * GROUP, GROUP)
            rows = pl.ds(start, GROUP)
            krows = pl.ds(pl.multiple_of(q * ROWS + start, GROUP), GROUP)
            w_re = unit_re[krows, :]
            w_im = unit_im[krows, :]
            mag = size[krows, :]
            a_re = jnp.zeros((GROUP, LANES), jnp.float32)
            a_im = jnp.zeros((GROUP, LANES), jnp.float32)
            e_sum = jnp.zeros((GROUP, LANES), jnp.float32)
            for tile in range(tiles):
                cols = pl.ds(tile * LANES, LANES)
                above = pl.ds((edge + tile + q) * LANES, LANES)
                below = pl.ds((edge + tile - q) * LANES, LANES)
                s_re = data[0, krows, cols].astype(jnp.float32)
                s_im = data[1, krows, cols].astype(jnp.float32)
                t_re = s_re * w_re + s_im * w_im
                t_im = s_im * w_re - s_re * w_im
                f_sum = fwd_sum[rows, above]
                f_im = fwd_im[rows, above]
                b_re = bwd_re[rows, below]
                b_sum = bwd_sum[rows, below]
                b_dif = bwd_dif[rows, below]
                shared = b_re * f_sum
                p_re = shared - f_im * b_dif
                p_im = shared - fwd_re[rows, above] * b_sum
                r_re = t_re - mag * p_re
                r_im = t_im - mag * p_im
                e_sum = e_sum + (r_re * r_re + r_im * r_im)
                a_re = a_re + (r_re * p_re + r_im * p_im)
                a_im = a_im + (r_im * p_re - r_re * p_im)
                x_re = mag * r_re
                x_im = mag * r_im
                x_sum = x_re + x_im
                shared = b_re * x_sum
                u_re = shared - x_im * b_sum
                u_im = shared - x_re * b_dif
                shared = f_im * x_sum
                d_re = shared + x_re * fwd_dif[rows, above]
                d_im = shared - x_im * f_sum
                if q == 0:
                    up_re[rows, above] = u_re
                    up_im[rows, above] = u_im
                    down_re[rows, below] = d_re
                    down_im[rows, below] = d_im
                else:
                    up_re[rows, above] += u_re
                    up_im[rows, above] += u_im
                    down_re[rows, below] += d_re
                    down_im[rows, below] += d_im
            part_re[krows, :] = a_re
            part_im[krows, :] = a_im
            err[...] += e_sum
            return carry

        lax.fori_loop(0, ROWS // GROUP, group, 0, unroll=UNROLL)

    ones = jnp.ones((8, LANES), jnp.float32)
    span = (owned + halo) // 2
    raised = []
    lowered = []
    for up, down in ((up_re, down_re), (up_im, down_im)):
        for half in range(2):
            first = halo - LANES + half * span
            total = up[0:8, first : first + span + LANES]
            for a in range(1, ROWS // 8):
                piece = up[8 * a : 8 * a + 8, first : first + span + LANES]
                total = total + pltpu.roll(piece, 8 * a, 1)
            raised.append(total)
            first = half * span
            total = down[0:8, first : first + span + LANES]
            for a in range(1, ROWS // 8):
                piece = down[8 * a : 8 * a + 8, first : first + span + LANES]
                total = total + pltpu.roll(piece, span + LANES - 8 * a, 1)
            lowered.append(total)
    raised = skew(jnp.concatenate(raised, axis=0), 1)[:, LANES:]
    lowered = skew(jnp.concatenate(lowered, axis=0), -1)[:, :span]
    raised = factor * jnp.sum(raised.reshape(4, 8, span), axis=1)
    lowered = factor * jnp.sum(lowered.reshape(4, 8, span), axis=1)
    for part in range(2):
        row = slice(part, part + 1)
        rise = jnp.concatenate([raised[2 * part + i : 2 * part + i + 1] for i in range(2)], axis=1)
        fall = jnp.concatenate([lowered[2 * part + i : 2 * part + i + 1] for i in range(2)], axis=1)
        out[row, 0:halo] = fall[:, :halo] * keep_low
        out[row, halo : halo + owned] = fall[:, halo:] + rise[:, :owned]
        out[row, halo + owned : width] = rise[:, owned:] * keep_high
    turned = [
        lax.dot_general(
            ones,
            sums[...],
            (((1,), (1,)), ((), ())),
            precision=lax.Precision.HIGHEST,
            preferred_element_type=jnp.float32,
        )[0:1, :]
        for sums in (part_re, part_im)
    ]
    line = turned[0] * turn_re - turned[1] * turn_im
    out[0:1, width : width + harmonics] = factor * line
    line = turned[0] * turn_im + turned[1] * turn_re
    out[1:2, width : width + harmonics] = factor * line
    out[0:1, width + harmonics :] = jnp.sum(err[...], axis=0, keepdims=True)
    out[1:2, width + harmonics :] = jnp.zeros((1, LANES), jnp.float32)


def local_gradients(factor, spectra, own, prof, prev, after):
    harmonics = prof.shape[1]
    owned = own.shape[1]
    width = owned + 2 * harmonics
    table = pltpu.VMEM((ROWS, width), jnp.float32)
    column = pltpu.VMEM((harmonics, LANES), jnp.float32)
    anywhere = pl.BlockSpec(memory_space=pltpu.HBM)
    inside = pl.BlockSpec(memory_space=pltpu.VMEM)
    return pl.pallas_call(
        functools.partial(gradient_kernel, factor),
        in_specs=[anywhere, anywhere, inside, inside, inside],
        out_specs=inside,
        out_shape=jax.ShapeDtypeStruct((2, width + harmonics + LANES), jnp.float32),
        scratch_shapes=[
            pltpu.VMEM((2, harmonics, owned), jnp.bfloat16),
            pltpu.VMEM((2, harmonics), jnp.float32),
        ]
        + [table] * 11
        + [column] * 5
        + [
            pltpu.VMEM((GROUP, LANES), jnp.float32),
            pltpu.SemaphoreType.DMA((harmonics // ROWS,)),
            pltpu.SemaphoreType.DMA,
        ],
        compiler_params=pltpu.CompilerParams(vmem_limit_bytes=VMEM_LIMIT),
    )(*(pltpu.with_memory_space_constraint(x, pltpu.HBM) for x in (spectra, prof)), own, prev, after)


def final_kernel(weight, sums, grads, low_add, high_add, filt, prof, filt_out, prof_out, misfit):
    harmonics = prof.shape[1]
    owned = filt.shape[1]
    halo = harmonics
    squares = jnp.sum(sums[:, harmonics + LANES :])
    scale = filter_rate / jnp.sqrt(jnp.full((2, LANES), squares) / (2 * CHANNELS) + epsilon)
    scale = scale[:, 0:1]
    low = grads[:, halo : 2 * halo] + low_add[:, halo:]
    middle = grads[:, 2 * halo : owned]
    high = grads[:, owned : owned + halo] + high_add[:, :halo]
    filt_out[:, :halo] = filt[:, :halo] - scale * low
    filt_out[:, halo : owned - halo] = filt[:, halo : owned - halo] - scale * middle
    filt_out[:, owned - halo :] = filt[:, owned - halo :] - scale * high
    grad = sums[:, :harmonics]
    mean = jnp.sum(grad * grad) / (2 * harmonics)
    rate = profile_rate / jnp.sqrt(jnp.full((2, LANES), mean) + epsilon)
    prof_out[...] = prof[...] - rate[:, 0:1] * grad
    total = jnp.sum(sums[:, harmonics : harmonics + LANES])
    misfit[0] = total * (weight / CHANNELS)


def update(weight, sums, grads, low_add, high_add, filt, prof):
    inside = pl.BlockSpec(memory_space=pltpu.VMEM)
    return pl.pallas_call(
        functools.partial(final_kernel, weight),
        in_specs=[inside] * 6,
        out_specs=[inside, inside, pl.BlockSpec(memory_space=pltpu.SMEM)],
        out_shape=[
            jax.ShapeDtypeStruct(filt.shape, jnp.float32),
            jax.ShapeDtypeStruct(prof.shape, jnp.float32),
            jax.ShapeDtypeStruct((1,), jnp.float32),
        ],
        compiler_params=pltpu.CompilerParams(vmem_limit_bytes=2 * 1024 * 1024),
    )(sums, grads, low_add, high_add, filt, prof)


def fold(values):
    total = values[:, :LANES]
    for start in range(LANES, values.shape[1], LANES):
        total = total + values[:, start : start + LANES]
    return total


def swap(values, axis, mask):
    count = lax.axis_size(axis)
    return lax.ppermute(values, axis, [(i, i ^ mask) for i in range(count)])


def neighbours(to_next, to_previous, axis):
    count = lax.axis_size(axis)
    ahead = [(i, (i + 1) % count) for i in range(count)]
    back = [(target, source) for source, target in ahead]
    return lax.ppermute(to_next, axis, ahead), lax.ppermute(to_previous, axis, back)


def join_blocks(sums, low_edge, high_edge, axis, masks):
    chan = lax.axis_index(axis)
    size = sums.shape[1]
    span = low_edge.shape[1]
    low_add = jnp.zeros_like(low_edge)
    high_add = jnp.zeros_like(high_edge)
    for step, mask in enumerate(masks):
        is_low = (chan >> step) & 1 == 0
        place = chan & ((1 << step) - 1)
        if step < len(masks) - 1:
            got = swap(jnp.concatenate([sums, low_edge, high_edge], axis=1), axis, mask)
            facing = jnp.where(is_low, got[:, size : size + span], got[:, size + span :])
        else:
            got = swap(jnp.concatenate([sums, jnp.where(is_low, high_edge, low_edge)], axis=1), axis, mask)
            facing = got[:, size:]
        mine = jnp.where(is_low, high_edge, low_edge)
        cross = 2.0 * fold(mine * facing)
        sums = sums + got[:, :size]
        sums = jnp.concatenate([sums[:, : size - LANES], sums[:, size - LANES :] + cross], axis=1)
        high_add = jnp.where(is_low & (place == (1 << step) - 1), facing, high_add)
        low_add = jnp.where(~is_low & (place == 0), facing, low_add)
        if step < len(masks) - 1:
            low_edge = jnp.where(is_low, low_edge, got[:, size : size + span])
            high_edge = jnp.where(is_low, got[:, size + span :], high_edge)
    return sums, low_add, high_add


def on_device(spectra, filter_init, profile_init):
    harmonics = profile_init.shape[1]
    owned = filter_init.shape[1]
    width = owned + 2 * harmonics
    weight = 1.0 / (lax.axis_size("sub") * spectra.shape[0] * harmonics)
    prev, after = neighbours(filter_init, filter_init, "chan")
    scale = jnp.where(lax.axis_index("chan") >= 0, 1.0, 0.0).astype(jnp.float32)
    own = filter_init * scale
    local = local_gradients(-2.0 * weight, spectra, own, profile_init, prev, after)
    for mask in (2, 6, 1):
        local = local + swap(local, "sub", mask)
    grads = local[:, :width]
    sums = jnp.concatenate([local[:, width:], fold(grads * grads)], axis=1)
    sums, low_add, high_add = join_blocks(
        sums, grads[:, : 2 * harmonics], grads[:, owned:], "chan", (1, 2, 4, 12)
    )
    return tuple(update(weight, sums, grads, low_add, high_add, filter_init, profile_init))


def solution(mesh):
    return jax.shard_map(
        on_device,
        mesh=mesh,
        in_specs=(P("sub", None, None, "chan"), P(None, "chan"), P()),
        out_specs=(P(None, "chan"), P(), P()),
        check_vma=False,
    )
```

```python
import functools

import jax
import jax.numpy as jnp
from jax import lax
from jax.experimental import pallas as pl
from jax.experimental.pallas import tpu as pltpu
from jax.sharding import PartitionSpec as P

CHANNELS = 32768
LANES = 128
ROWS = 128
GROUP = 16
UNROLL = 8
VMEM_LIMIT = 28 * 1024 * 1024

filter_rate = 0.1
profile_rate = 0.1
epsilon = 1e-06


def skew(block, sign):
    width = block.shape[1]
    row = lax.broadcasted_iota(jnp.int32, block.shape, 0)
    for bit in (1, 2, 4):
        moved = pltpu.roll(block, bit if sign > 0 else width - bit, 1)
        block = jnp.where((row & bit) != 0, moved, block)
    return block


def gradient_kernel(
    factor, spectra, prof, own, prev, after, out,
    data, fwd_re, fwd_im, fwd_sum, fwd_dif, bwd_re, bwd_sum, bwd_dif,
    up_re, up_im, down_re, down_im,
    unit_re, unit_im, size, part_re, part_im, err, block_sems,
):
    owned = own.shape[1]
    harmonics = prof.shape[1]
    halo = harmonics
    width = owned + 2 * halo
    blocks = harmonics // ROWS
    edge = halo // LANES
    tiles = owned // LANES
    chan = lax.axis_index("chan")
    last = lax.axis_size("chan") - 1
    copies = [
        pltpu.make_async_copy(
            spectra.at[0, :, pl.ds(q * ROWS, ROWS), :],
            data.at[:, pl.ds(q * ROWS, ROWS), :],
            block_sems.at[q],
        )
        for q in range(blocks)
    ]
    for copy in copies:
        copy.start()

    for acc in (up_re, up_im):
        acc[:, halo - LANES : halo] = jnp.zeros((ROWS, LANES), jnp.float32)
        acc[:, halo + owned :] = jnp.zeros((ROWS, halo), jnp.float32)
    for acc in (down_re, down_im):
        acc[:, :halo] = jnp.zeros((ROWS, halo), jnp.float32)
        acc[:, halo + owned : halo + owned + LANES] = jnp.zeros((ROWS, LANES), jnp.float32)

    keep_low = jnp.where(chan == 0, 0.0, 1.0).astype(jnp.float32)
    keep_high = jnp.where(chan == last, 0.0, 1.0).astype(jnp.float32)
    reach = halo - ROWS
    lines = [
        jnp.concatenate(
            [
                prev[part : part + 1, owned - halo :] * keep_low,
                own[part : part + 1, :],
                after[part : part + 1, :halo] * keep_high,
            ],
            axis=1,
        )
        for part in range(2)
    ]
    bases = [jnp.broadcast_to(line, (8, width)) for line in lines]
    rights = [skew(base, 1) for base in bases]
    lefts = [skew(base, -1) for base in bases]
    behind = slice(halo - reach, halo + owned)
    ahead = slice(halo, halo + owned + reach)
    for a in range(ROWS // 8):
        rows = pl.ds(8 * a, 8)
        re, im = ((pltpu.roll(x, 8 * a, 1) if a else x)[:, behind] for x in rights)
        bwd_re[rows, behind] = re
        bwd_sum[rows, behind] = re + im
        bwd_dif[rows, behind] = re - im
        re, im = ((pltpu.roll(x, width - 8 * a, 1) if a else x)[:, ahead] for x in lefts)
        fwd_re[rows, ahead] = re
        fwd_im[rows, ahead] = im
        fwd_sum[rows, ahead] = re + im
        fwd_dif[rows, ahead] = re - im

    prof_re = prof[0:1, :]
    prof_im = prof[1:2, :]
    length = jnp.sqrt(prof_re * prof_re + prof_im * prof_im)
    present = length > 0.0
    divisor = jnp.where(present, length, 1.0)
    turn_re = jnp.where(present, prof_re / divisor, 1.0)
    turn_im = jnp.where(present, prof_im / divisor, 0.0)
    columns = jnp.transpose(
        jnp.concatenate([turn_re, turn_im, length, jnp.zeros((5, harmonics), jnp.float32)], axis=0)
    )
    for index, table in enumerate((unit_re, unit_im, size)):
        table[...] = jnp.broadcast_to(columns[:, index : index + 1], (harmonics, LANES))
    err[...] = jnp.zeros_like(err)

    for q in range(blocks):
        copies[q].wait()

        def group(index, carry, q=q):
            start = pl.multiple_of(index * GROUP, GROUP)
            rows = pl.ds(start, GROUP)
            krows = pl.ds(pl.multiple_of(q * ROWS + start, GROUP), GROUP)
            w_re = unit_re[krows, :]
            w_im = unit_im[krows, :]
            mag = size[krows, :]
            a_re = jnp.zeros((GROUP, LANES), jnp.float32)
            a_im = jnp.zeros((GROUP, LANES), jnp.float32)
            e_sum = jnp.zeros((GROUP, LANES), jnp.float32)
            for tile in range(tiles):
                cols = pl.ds(tile * LANES, LANES)
                above = pl.ds((edge + tile + q) * LANES, LANES)
                below = pl.ds((edge + tile - q) * LANES, LANES)
                s_re = data[0, krows, cols].astype(jnp.float32)
                s_im = data[1, krows, cols].astype(jnp.float32)
                t_re = s_re * w_re + s_im * w_im
                t_im = s_im * w_re - s_re * w_im
                f_sum = fwd_sum[rows, above]
                f_im = fwd_im[rows, above]
                b_re = bwd_re[rows, below]
                b_sum = bwd_sum[rows, below]
                b_dif = bwd_dif[rows, below]
                shared = b_re * f_sum
                p_re = shared - f_im * b_dif
                p_im = shared - fwd_re[rows, above] * b_sum
                r_re = t_re - mag * p_re
                r_im = t_im - mag * p_im
                e_sum = e_sum + (r_re * r_re + r_im * r_im)
                a_re = a_re + (r_re * p_re + r_im * p_im)
                a_im = a_im + (r_im * p_re - r_re * p_im)
                x_re = mag * r_re
                x_im = mag * r_im
                x_sum = x_re + x_im
                shared = b_re * x_sum
                u_re = shared - x_im * b_sum
                u_im = shared - x_re * b_dif
                shared = f_im * x_sum
                d_re = shared + x_re * fwd_dif[rows, above]
                d_im = shared - x_im * f_sum
                if q == 0:
                    up_re[rows, above] = u_re
                    up_im[rows, above] = u_im
                    down_re[rows, below] = d_re
                    down_im[rows, below] = d_im
                else:
                    up_re[rows, above] += u_re
                    up_im[rows, above] += u_im
                    down_re[rows, below] += d_re
                    down_im[rows, below] += d_im
            part_re[krows, :] = a_re
            part_im[krows, :] = a_im
            err[...] += e_sum
            return carry

        lax.fori_loop(0, ROWS // GROUP, group, 0, unroll=UNROLL)

    ones = jnp.ones((8, LANES), jnp.float32)
    span = (owned + halo) // 2
    raised = []
    lowered = []
    for up, down in ((up_re, down_re), (up_im, down_im)):
        for half in range(2):
            first = halo - LANES + half * span
            total = up[0:8, first : first + span + LANES]
            for a in range(1, ROWS // 8):
                piece = up[8 * a : 8 * a + 8, first : first + span + LANES]
                total = total + pltpu.roll(piece, 8 * a, 1)
            raised.append(total)
            first = half * span
            total = down[0:8, first : first + span + LANES]
            for a in range(1, ROWS // 8):
                piece = down[8 * a : 8 * a + 8, first : first + span + LANES]
                total = total + pltpu.roll(piece, span + LANES - 8 * a, 1)
            lowered.append(total)
    raised = skew(jnp.concatenate(raised, axis=0), 1)[:, LANES:]
    lowered = skew(jnp.concatenate(lowered, axis=0), -1)[:, :span]
    raised = factor * jnp.sum(raised.reshape(4, 8, span), axis=1)
    lowered = factor * jnp.sum(lowered.reshape(4, 8, span), axis=1)
    for part in range(2):
        row = slice(part, part + 1)
        rise = jnp.concatenate([raised[2 * part + i : 2 * part + i + 1] for i in range(2)], axis=1)
        fall = jnp.concatenate([lowered[2 * part + i : 2 * part + i + 1] for i in range(2)], axis=1)
        out[row, 0:halo] = fall[:, :halo] * keep_low
        out[row, halo : halo + owned] = fall[:, halo:] + rise[:, :owned]
        out[row, halo + owned : width] = rise[:, owned:] * keep_high
    turned = [
        lax.dot_general(
            ones,
            sums[...],
            (((1,), (1,)), ((), ())),
            precision=lax.Precision.HIGHEST,
            preferred_element_type=jnp.float32,
        )[0:1, :]
        for sums in (part_re, part_im)
    ]
    line = turned[0] * turn_re - turned[1] * turn_im
    out[0:1, width : width + harmonics] = factor * line
    line = turned[0] * turn_im + turned[1] * turn_re
    out[1:2, width : width + harmonics] = factor * line
    out[0:1, width + harmonics :] = jnp.sum(err[...], axis=0, keepdims=True)
    out[1:2, width + harmonics :] = jnp.zeros((1, LANES), jnp.float32)


def local_gradients(factor, spectra, own, prof, prev, after):
    harmonics = prof.shape[1]
    owned = own.shape[1]
    width = owned + 2 * harmonics
    table = pltpu.VMEM((ROWS, width), jnp.float32)
    column = pltpu.VMEM((harmonics, LANES), jnp.float32)
    anywhere = pl.BlockSpec(memory_space=pltpu.HBM)
    inside = pl.BlockSpec(memory_space=pltpu.VMEM)
    return pl.pallas_call(
        functools.partial(gradient_kernel, factor),
        in_specs=[anywhere, inside, inside, inside, inside],
        out_specs=inside,
        out_shape=jax.ShapeDtypeStruct((2, width + harmonics + LANES), jnp.float32),
        scratch_shapes=[
            pltpu.VMEM((2, harmonics, owned), jnp.bfloat16),
        ]
        + [table] * 11
        + [column] * 5
        + [
            pltpu.VMEM((GROUP, LANES), jnp.float32),
            pltpu.SemaphoreType.DMA((harmonics // ROWS,)),
        ],
        compiler_params=pltpu.CompilerParams(vmem_limit_bytes=VMEM_LIMIT),
    )(pltpu.with_memory_space_constraint(spectra, pltpu.HBM), prof, own, prev, after)


def final_kernel(weight, sums, grads, low_add, high_add, filt, prof, filt_out, prof_out, misfit):
    harmonics = prof.shape[1]
    owned = filt.shape[1]
    halo = harmonics
    squares = jnp.sum(sums[:, harmonics + LANES :])
    scale = filter_rate / jnp.sqrt(jnp.full((2, LANES), squares) / (2 * CHANNELS) + epsilon)
    scale = scale[:, 0:1]
    low = grads[:, halo : 2 * halo] + low_add[:, halo:]
    middle = grads[:, 2 * halo : owned]
    high = grads[:, owned : owned + halo] + high_add[:, :halo]
    filt_out[:, :halo] = filt[:, :halo] - scale * low
    filt_out[:, halo : owned - halo] = filt[:, halo : owned - halo] - scale * middle
    filt_out[:, owned - halo :] = filt[:, owned - halo :] - scale * high
    grad = sums[:, :harmonics]
    mean = jnp.sum(grad * grad) / (2 * harmonics)
    rate = profile_rate / jnp.sqrt(jnp.full((2, LANES), mean) + epsilon)
    prof_out[...] = prof[...] - rate[:, 0:1] * grad
    total = jnp.sum(sums[:, harmonics : harmonics + LANES])
    misfit[0] = total * (weight / CHANNELS)


def update(weight, sums, grads, low_add, high_add, filt, prof):
    inside = pl.BlockSpec(memory_space=pltpu.VMEM)
    return pl.pallas_call(
        functools.partial(final_kernel, weight),
        in_specs=[inside] * 6,
        out_specs=[inside, inside, pl.BlockSpec(memory_space=pltpu.SMEM)],
        out_shape=[
            jax.ShapeDtypeStruct(filt.shape, jnp.float32),
            jax.ShapeDtypeStruct(prof.shape, jnp.float32),
            jax.ShapeDtypeStruct((1,), jnp.float32),
        ],
        compiler_params=pltpu.CompilerParams(vmem_limit_bytes=2 * 1024 * 1024),
    )(sums, grads, low_add, high_add, filt, prof)


def fold(values):
    total = values[:, :LANES]
    for start in range(LANES, values.shape[1], LANES):
        total = total + values[:, start : start + LANES]
    return total


def swap(values, axis, mask):
    count = lax.axis_size(axis)
    return lax.ppermute(values, axis, [(i, i ^ mask) for i in range(count)])


def neighbours(to_next, to_previous, axis):
    count = lax.axis_size(axis)
    ahead = [(i, (i + 1) % count) for i in range(count)]
    back = [(target, source) for source, target in ahead]
    return lax.ppermute(to_next, axis, ahead), lax.ppermute(to_previous, axis, back)


def join_blocks(sums, low_edge, high_edge, axis, masks):
    chan = lax.axis_index(axis)
    size = sums.shape[1]
    span = low_edge.shape[1]
    low_add = jnp.zeros_like(low_edge)
    high_add = jnp.zeros_like(high_edge)
    for step, mask in enumerate(masks):
        is_low = (chan >> step) & 1 == 0
        place = chan & ((1 << step) - 1)
        if step < len(masks) - 1:
            got = swap(jnp.concatenate([sums, low_edge, high_edge], axis=1), axis, mask)
            facing = jnp.where(is_low, got[:, size : size + span], got[:, size + span :])
        else:
            got = swap(jnp.concatenate([sums, jnp.where(is_low, high_edge, low_edge)], axis=1), axis, mask)
            facing = got[:, size:]
        mine = jnp.where(is_low, high_edge, low_edge)
        cross = 2.0 * fold(mine * facing)
        sums = sums + got[:, :size]
        sums = jnp.concatenate([sums[:, : size - LANES], sums[:, size - LANES :] + cross], axis=1)
        high_add = jnp.where(is_low & (place == (1 << step) - 1), facing, high_add)
        low_add = jnp.where(~is_low & (place == 0), facing, low_add)
        if step < len(masks) - 1:
            low_edge = jnp.where(is_low, low_edge, got[:, size : size + span])
            high_edge = jnp.where(is_low, got[:, size + span :], high_edge)
    return sums, low_add, high_add


def on_device(spectra, filter_init, profile_init):
    harmonics = profile_init.shape[1]
    owned = filter_init.shape[1]
    width = owned + 2 * harmonics
    weight = 1.0 / (lax.axis_size("sub") * spectra.shape[0] * harmonics)
    prev, after = neighbours(filter_init, filter_init, "chan")
    scale = jnp.where(lax.axis_index("chan") >= 0, 1.0, 0.0).astype(jnp.float32)
    own = filter_init * scale
    local = local_gradients(-2.0 * weight, spectra, own, profile_init * scale, prev, after)
    for mask in (2, 6, 1):
        local = local + swap(local, "sub", mask)
    grads = local[:, :width]
    sums = jnp.concatenate([local[:, width:], fold(grads * grads)], axis=1)
    sums, low_add, high_add = join_blocks(
        sums, grads[:, : 2 * harmonics], grads[:, owned:], "chan", (1, 2, 4, 12)
    )
    return tuple(update(weight, sums, grads, low_add, high_add, filter_init, profile_init))


def solution(mesh):
    return jax.shard_map(
        on_device,
        mesh=mesh,
        in_specs=(P("sub", None, None, "chan"), P(None, "chan"), P()),
        out_specs=(P(None, "chan"), P(), P()),
        check_vma=False,
    )
```

```python
import functools

import jax
import jax.numpy as jnp
from jax import lax
from jax.experimental import pallas as pl
from jax.experimental.pallas import tpu as pltpu
from jax.sharding import PartitionSpec as P

CHANNELS = 32768
LANES = 128
ROWS = 128
GROUP = 16
UNROLL = 8
VMEM_LIMIT = 40 * 1024 * 1024

filter_rate = 0.1
profile_rate = 0.1
epsilon = 1e-06


def skew(block, sign):
    width = block.shape[1]
    if sign > 0 and block.shape[0] == 8:
        return pltpu.roll(block, 0, 1, stride=1, stride_axis=0)
    row = lax.broadcasted_iota(jnp.int32, block.shape, 0)
    for bit in (1, 2, 4):
        moved = pltpu.roll(block, bit if sign > 0 else width - bit, 1)
        block = jnp.where((row & bit) != 0, moved, block)
    return block


def gradient_kernel(
    factor, spectra, prof, own, prev, after, out,
    data, fwd_re, fwd_im, fwd_sum, fwd_dif, bwd_re, bwd_sum, bwd_dif,
    up_re, up_im, down_re, down_im,
    unit_re, unit_im, size, part_re, part_im, err, block_sems,
):
    owned = own.shape[1]
    harmonics = prof.shape[1]
    halo = harmonics
    width = owned + 2 * halo
    blocks = harmonics // ROWS
    edge = halo // LANES
    tiles = owned // LANES
    chan = lax.axis_index("chan")
    last = lax.axis_size("chan") - 1
    copies = [
        pltpu.make_async_copy(
            spectra.at[0, :, pl.ds(q * ROWS, ROWS), :],
            data.at[:, pl.ds(q * ROWS, ROWS), :],
            block_sems.at[q],
        )
        for q in range(blocks)
    ]
    copies[0].start()

    for acc in (up_re, up_im):
        acc[:, halo - LANES : halo] = jnp.zeros((ROWS, LANES), jnp.float32)
        acc[:, halo + owned :] = jnp.zeros((ROWS, halo), jnp.float32)
    for acc in (down_re, down_im):
        acc[:, :halo] = jnp.zeros((ROWS, halo), jnp.float32)
        acc[:, halo + owned : halo + owned + LANES] = jnp.zeros((ROWS, LANES), jnp.float32)

    keep_low = jnp.where(chan == 0, 0.0, 1.0).astype(jnp.float32)
    keep_high = jnp.where(chan == last, 0.0, 1.0).astype(jnp.float32)
    reach = halo - ROWS
    lines = [
        jnp.concatenate(
            [
                prev[part : part + 1, owned - halo :] * keep_low,
                own[part : part + 1, :],
                after[part : part + 1, :halo] * keep_high,
            ],
            axis=1,
        )
        for part in range(2)
    ]
    bases = [jnp.broadcast_to(line, (8, width)) for line in lines]
    rights = [skew(base, 1) for base in bases]
    lefts = [skew(base, -1) for base in bases]
    behind = slice(halo - reach, halo + owned)
    ahead = slice(halo, halo + owned + reach)
    for a in range(ROWS // 8):
        rows = pl.ds(8 * a, 8)
        re, im = ((pltpu.roll(x, 8 * a, 1) if a else x)[:, behind] for x in rights)
        bwd_re[rows, behind] = re
        bwd_sum[rows, behind] = re + im
        bwd_dif[rows, behind] = re - im
        re, im = ((pltpu.roll(x, width - 8 * a, 1) if a else x)[:, ahead] for x in lefts)
        fwd_re[rows, ahead] = re
        fwd_im[rows, ahead] = im
        fwd_sum[rows, ahead] = re + im
        fwd_dif[rows, ahead] = re - im

    prof_re = prof[0:1, :]
    prof_im = prof[1:2, :]
    length = jnp.sqrt(prof_re * prof_re + prof_im * prof_im)
    present = length > 0.0
    divisor = jnp.where(present, length, 1.0)
    turn_re = jnp.where(present, prof_re / divisor, 1.0)
    turn_im = jnp.where(present, prof_im / divisor, 0.0)
    columns = jnp.transpose(
        jnp.concatenate([turn_re, turn_im, length, jnp.zeros((5, harmonics), jnp.float32)], axis=0)
    )
    for index, table in enumerate((unit_re, unit_im, size)):
        table[...] = jnp.broadcast_to(columns[:, index : index + 1], (harmonics, LANES))
    err[...] = jnp.zeros_like(err)

    for q in range(blocks):
        copies[q].wait()
        if q == 0:
            for copy in copies[1:]:
                copy.start()

        def group(index, carry, q=q):
            start = pl.multiple_of(index * GROUP, GROUP)
            rows = pl.ds(start, GROUP)
            krows = pl.ds(pl.multiple_of(q * ROWS + start, GROUP), GROUP)
            w_re = unit_re[krows, :]
            w_im = unit_im[krows, :]
            mag = size[krows, :]
            a_re = jnp.zeros((GROUP, LANES), jnp.float32)
            a_im = jnp.zeros((GROUP, LANES), jnp.float32)
            e_sum = jnp.zeros((GROUP, LANES), jnp.float32)
            for tile in range(tiles):
                cols = pl.ds(tile * LANES, LANES)
                above = pl.ds((edge + tile + q) * LANES, LANES)
                below = pl.ds((edge + tile - q) * LANES, LANES)
                s_re = data[0, krows, cols].astype(jnp.float32)
                s_im = data[1, krows, cols].astype(jnp.float32)
                t_re = s_re * w_re + s_im * w_im
                t_im = s_im * w_re - s_re * w_im
                f_sum = fwd_sum[rows, above]
                f_im = fwd_im[rows, above]
                b_re = bwd_re[rows, below]
                b_sum = bwd_sum[rows, below]
                b_dif = bwd_dif[rows, below]
                shared = b_re * f_sum
                p_re = shared - f_im * b_dif
                p_im = shared - fwd_re[rows, above] * b_sum
                r_re = t_re - mag * p_re
                r_im = t_im - mag * p_im
                e_sum = e_sum + (r_re * r_re + r_im * r_im)
                a_re = a_re + (r_re * p_re + r_im * p_im)
                a_im = a_im + (r_im * p_re - r_re * p_im)
                x_re = mag * r_re
                x_im = mag * r_im
                x_sum = x_re + x_im
                shared = b_re * x_sum
                u_re = shared - x_im * b_sum
                u_im = shared - x_re * b_dif
                shared = f_im * x_sum
                d_re = shared + x_re * fwd_dif[rows, above]
                d_im = shared - x_im * f_sum
                if q == 0:
                    up_re[rows, above] = u_re
                    up_im[rows, above] = u_im
                    down_re[rows, below] = d_re
                    down_im[rows, below] = d_im
                else:
                    up_re[rows, above] += u_re
                    up_im[rows, above] += u_im
                    down_re[rows, below] += d_re
                    down_im[rows, below] += d_im
            part_re[krows, :] = a_re
            part_im[krows, :] = a_im
            err[...] += e_sum
            return carry

        lax.fori_loop(0, ROWS // GROUP, group, 0, unroll=UNROLL)

    ones = jnp.ones((8, LANES), jnp.float32)
    pieces = 4
    span = (owned + halo) // pieces
    raised = [[], []]
    lowered = [[], []]
    for piece in range(pieces):
        high = slice(halo - LANES + piece * span, halo + piece * span + span)
        low = slice(piece * span, piece * span + span + LANES)
        totals = [jnp.zeros((8, span + LANES), jnp.float32)] * 4
        for a in range(ROWS // 8):
            rows = slice(8 * a, 8 * a + 8)
            back = span + LANES - 8 * a
            totals[0] = totals[0] + pltpu.roll(up_re[rows, high], 8 * a, 1, stride=1, stride_axis=0)
            totals[1] = totals[1] + pltpu.roll(up_im[rows, high], 8 * a, 1, stride=1, stride_axis=0)
            totals[2] = totals[2] + (pltpu.roll(down_re[rows, low], back, 1) if a else down_re[rows, low])
            totals[3] = totals[3] + (pltpu.roll(down_im[rows, low], back, 1) if a else down_im[rows, low])
        for part in range(2):
            raised[part].append(totals[part][:, LANES:])
            lowered[part].append(totals[2 + part])
    raised = jnp.concatenate(raised[0] + raised[1], axis=0)
    lowered = skew(jnp.concatenate(lowered[0] + lowered[1], axis=0), -1)[:, :span]
    raised = factor * jnp.sum(raised.reshape(2 * pieces, 8, span), axis=1)
    lowered = factor * jnp.sum(lowered.reshape(2 * pieces, 8, span), axis=1)
    for part in range(2):
        row = slice(part, part + 1)
        rise = jnp.concatenate([raised[pieces * part + i : pieces * part + i + 1] for i in range(pieces)], axis=1)
        fall = jnp.concatenate([lowered[pieces * part + i : pieces * part + i + 1] for i in range(pieces)], axis=1)
        out[row, 0:halo] = fall[:, :halo] * keep_low
        out[row, halo : halo + owned] = fall[:, halo:] + rise[:, :owned]
        out[row, halo + owned : width] = rise[:, owned:] * keep_high
    turned = [
        lax.dot_general(
            ones,
            sums[...],
            (((1,), (1,)), ((), ())),
            precision=lax.Precision.HIGHEST,
            preferred_element_type=jnp.float32,
        )[0:1, :]
        for sums in (part_re, part_im)
    ]
    line = turned[0] * turn_re - turned[1] * turn_im
    out[0:1, width : width + harmonics] = factor * line
    line = turned[0] * turn_im + turned[1] * turn_re
    out[1:2, width : width + harmonics] = factor * line
    out[0:1, width + harmonics :] = jnp.sum(err[...], axis=0, keepdims=True)
    out[1:2, width + harmonics :] = jnp.zeros((1, LANES), jnp.float32)


def local_gradients(factor, spectra, own, prof, prev, after):
    harmonics = prof.shape[1]
    owned = own.shape[1]
    width = owned + 2 * harmonics
    table = pltpu.VMEM((ROWS, width), jnp.float32)
    column = pltpu.VMEM((harmonics, LANES), jnp.float32)
    anywhere = pl.BlockSpec(memory_space=pltpu.HBM)
    inside = pl.BlockSpec(memory_space=pltpu.VMEM)
    return pl.pallas_call(
        functools.partial(gradient_kernel, factor),
        in_specs=[anywhere, inside, inside, inside, inside],
        out_specs=inside,
        out_shape=jax.ShapeDtypeStruct((2, width + harmonics + LANES), jnp.float32),
        scratch_shapes=[
            pltpu.VMEM((2, harmonics, owned), jnp.bfloat16),
        ]
        + [table] * 11
        + [column] * 5
        + [
            pltpu.VMEM((GROUP, LANES), jnp.float32),
            pltpu.SemaphoreType.DMA((harmonics // ROWS,)),
        ],
        compiler_params=pltpu.CompilerParams(vmem_limit_bytes=VMEM_LIMIT),
    )(pltpu.with_memory_space_constraint(spectra, pltpu.HBM), prof, own, prev, after)


def final_kernel(weight, sums, grads, low_add, high_add, filt, prof, filt_out, prof_out, misfit):
    harmonics = prof.shape[1]
    owned = filt.shape[1]
    halo = harmonics
    squares = jnp.sum(sums[:, harmonics + LANES :])
    scale = filter_rate / jnp.sqrt(jnp.full((2, LANES), squares) / (2 * CHANNELS) + epsilon)
    scale = scale[:, 0:1]
    low = grads[:, halo : 2 * halo] + low_add[:, halo:]
    middle = grads[:, 2 * halo : owned]
    high = grads[:, owned : owned + halo] + high_add[:, :halo]
    filt_out[:, :halo] = filt[:, :halo] - scale * low
    filt_out[:, halo : owned - halo] = filt[:, halo : owned - halo] - scale * middle
    filt_out[:, owned - halo :] = filt[:, owned - halo :] - scale * high
    grad = sums[:, :harmonics]
    mean = jnp.sum(grad * grad) / (2 * harmonics)
    rate = profile_rate / jnp.sqrt(jnp.full((2, LANES), mean) + epsilon)
    prof_out[...] = prof[...] - rate[:, 0:1] * grad
    total = jnp.sum(sums[:, harmonics : harmonics + LANES])
    misfit[0] = total * (weight / CHANNELS)


def update(weight, sums, grads, low_add, high_add, filt, prof):
    inside = pl.BlockSpec(memory_space=pltpu.VMEM)
    return pl.pallas_call(
        functools.partial(final_kernel, weight),
        in_specs=[inside] * 6,
        out_specs=[inside, inside, pl.BlockSpec(memory_space=pltpu.SMEM)],
        out_shape=[
            jax.ShapeDtypeStruct(filt.shape, jnp.float32),
            jax.ShapeDtypeStruct(prof.shape, jnp.float32),
            jax.ShapeDtypeStruct((1,), jnp.float32),
        ],
        compiler_params=pltpu.CompilerParams(vmem_limit_bytes=2 * 1024 * 1024),
    )(sums, grads, low_add, high_add, filt, prof)


def fold(values):
    total = values[:, :LANES]
    for start in range(LANES, values.shape[1], LANES):
        total = total + values[:, start : start + LANES]
    return total


def swap(values, axis, mask):
    count = lax.axis_size(axis)
    return lax.ppermute(values, axis, [(i, i ^ mask) for i in range(count)])


def neighbours(to_next, to_previous, axis):
    count = lax.axis_size(axis)
    ahead = [(i, (i + 1) % count) for i in range(count)]
    back = [(target, source) for source, target in ahead]
    return lax.ppermute(to_next, axis, ahead), lax.ppermute(to_previous, axis, back)


def join_blocks(sums, low_edge, high_edge, axis, masks):
    chan = lax.axis_index(axis)
    size = sums.shape[1]
    span = low_edge.shape[1]
    low_add = jnp.zeros_like(low_edge)
    high_add = jnp.zeros_like(high_edge)
    for step, mask in enumerate(masks):
        is_low = (chan >> step) & 1 == 0
        place = chan & ((1 << step) - 1)
        if step < len(masks) - 1:
            got = swap(jnp.concatenate([sums, low_edge, high_edge], axis=1), axis, mask)
            facing = jnp.where(is_low, got[:, size : size + span], got[:, size + span :])
        else:
            got = swap(jnp.concatenate([sums, jnp.where(is_low, high_edge, low_edge)], axis=1), axis, mask)
            facing = got[:, size:]
        mine = jnp.where(is_low, high_edge, low_edge)
        cross = 2.0 * fold(mine * facing)
        sums = sums + got[:, :size]
        sums = jnp.concatenate([sums[:, : size - LANES], sums[:, size - LANES :] + cross], axis=1)
        high_add = jnp.where(is_low & (place == (1 << step) - 1), facing, high_add)
        low_add = jnp.where(~is_low & (place == 0), facing, low_add)
        if step < len(masks) - 1:
            low_edge = jnp.where(is_low, low_edge, got[:, size : size + span])
            high_edge = jnp.where(is_low, got[:, size + span :], high_edge)
    return sums, low_add, high_add


def on_device(spectra, filter_init, profile_init):
    harmonics = profile_init.shape[1]
    owned = filter_init.shape[1]
    width = owned + 2 * harmonics
    weight = 1.0 / (lax.axis_size("sub") * spectra.shape[0] * harmonics)
    prev, after = neighbours(filter_init, filter_init, "chan")
    scale = jnp.where(lax.axis_index("chan") >= 0, 1.0, 0.0).astype(jnp.float32)
    own = filter_init * scale
    local = local_gradients(-2.0 * weight, spectra, own, profile_init * scale, prev, after)
    for mask in (2, 6, 1):
        local = local + swap(local, "sub", mask)
    grads = local[:, :width]
    sums = jnp.concatenate([local[:, width:], fold(grads * grads)], axis=1)
    sums, low_add, high_add = join_blocks(
        sums, grads[:, : 2 * harmonics], grads[:, owned:], "chan", (1, 2, 4, 12)
    )
    return tuple(update(weight, sums, grads, low_add, high_add, filter_init, profile_init))


def solution(mesh):
    return jax.shard_map(
        on_device,
        mesh=mesh,
        in_specs=(P("sub", None, None, "chan"), P(None, "chan"), P()),
        out_specs=(P(None, "chan"), P(), P()),
        check_vma=False,
    )
```

```python
import functools

import jax
import jax.numpy as jnp
from jax import lax
from jax.experimental import pallas as pl
from jax.experimental.pallas import tpu as pltpu
from jax.sharding import PartitionSpec as P

CHANNELS = 32768
LANES = 128
ROWS = 128
GROUP = 16
UNROLL = 8
VMEM_LIMIT = 40 * 1024 * 1024

filter_rate = 0.1
profile_rate = 0.1
epsilon = 1e-06


def skew(block, sign):
    width = block.shape[1]
    if sign > 0 and block.shape[0] == 8:
        return pltpu.roll(block, 0, 1, stride=1, stride_axis=0)
    row = lax.broadcasted_iota(jnp.int32, block.shape, 0)
    for bit in (1, 2, 4):
        moved = pltpu.roll(block, bit if sign > 0 else width - bit, 1)
        block = jnp.where((row & bit) != 0, moved, block)
    return block


def gradient_kernel(
    factor, spectra, prof, own, prev, after, out,
    data, fwd_re, fwd_im, fwd_sum, fwd_dif, bwd_re, bwd_sum, bwd_dif,
    up_re, up_im, down_re, down_im,
    unit_re, unit_im, size, part_re, part_im, err, block_sems,
):
    owned = own.shape[1]
    harmonics = prof.shape[1]
    halo = harmonics
    width = owned + 2 * halo
    blocks = harmonics // ROWS
    edge = halo // LANES
    tiles = owned // LANES
    chan = lax.axis_index("chan")
    last = lax.axis_size("chan") - 1
    copies = [
        pltpu.make_async_copy(
            spectra.at[0, :, pl.ds(q * ROWS, ROWS), :],
            data.at[:, pl.ds(q * ROWS, ROWS), :],
            block_sems.at[q],
        )
        for q in range(blocks)
    ]
    copies[0].start()

    for acc in (up_re, up_im):
        acc[:, halo - LANES : halo] = jnp.zeros((ROWS, LANES), jnp.float32)
        acc[:, halo + owned :] = jnp.zeros((ROWS, halo), jnp.float32)
    for acc in (down_re, down_im):
        acc[:, :halo] = jnp.zeros((ROWS, halo), jnp.float32)
        acc[:, halo + owned : halo + owned + LANES] = jnp.zeros((ROWS, LANES), jnp.float32)

    keep_low = jnp.where(chan == 0, 0.0, 1.0).astype(jnp.float32)
    keep_high = jnp.where(chan == last, 0.0, 1.0).astype(jnp.float32)
    reach = halo - ROWS
    lines = [
        jnp.concatenate(
            [
                prev[part : part + 1, owned - halo :] * keep_low,
                own[part : part + 1, :],
                after[part : part + 1, :halo] * keep_high,
            ],
            axis=1,
        )
        for part in range(2)
    ]
    bases = [jnp.broadcast_to(line, (8, width)) for line in lines]
    rights = [skew(base, 1) for base in bases]
    lefts = [skew(base, -1) for base in bases]
    behind = slice(halo - reach, halo + owned)
    ahead = slice(halo, halo + owned + reach)
    for a in range(ROWS // 8):
        rows = pl.ds(8 * a, 8)
        re, im = ((pltpu.roll(x, 8 * a, 1) if a else x)[:, behind] for x in rights)
        bwd_re[rows, behind] = re
        bwd_sum[rows, behind] = re + im
        bwd_dif[rows, behind] = re - im
        re, im = ((pltpu.roll(x, width - 8 * a, 1) if a else x)[:, ahead] for x in lefts)
        fwd_re[rows, ahead] = re
        fwd_im[rows, ahead] = im
        fwd_sum[rows, ahead] = re + im
        fwd_dif[rows, ahead] = re - im

    prof_re = prof[0:1, :]
    prof_im = prof[1:2, :]
    length = jnp.sqrt(prof_re * prof_re + prof_im * prof_im)
    present = length > 0.0
    divisor = jnp.where(present, length, 1.0)
    turn_re = jnp.where(present, prof_re / divisor, 1.0)
    turn_im = jnp.where(present, prof_im / divisor, 0.0)
    columns = jnp.transpose(
        jnp.concatenate([turn_re, turn_im, length, jnp.zeros((5, harmonics), jnp.float32)], axis=0)
    )
    for index, table in enumerate((unit_re, unit_im, size)):
        table[...] = jnp.broadcast_to(columns[:, index : index + 1], (harmonics, LANES))
    err[...] = jnp.zeros_like(err)

    for q in range(blocks):
        copies[q].wait()
        if q == 0:
            for copy in copies[1:]:
                copy.start()

        def group(index, carry, q=q):
            start = pl.multiple_of(index * GROUP, GROUP)
            rows = pl.ds(start, GROUP)
            krows = pl.ds(pl.multiple_of(q * ROWS + start, GROUP), GROUP)
            w_re = unit_re[krows, :]
            w_im = unit_im[krows, :]
            mag = size[krows, :]
            a_re = jnp.zeros((GROUP, LANES), jnp.float32)
            a_im = jnp.zeros((GROUP, LANES), jnp.float32)
            e_sum = err[...]
            for tile in range(tiles):
                cols = pl.ds(tile * LANES, LANES)
                above = pl.ds((edge + tile + q) * LANES, LANES)
                below = pl.ds((edge + tile - q) * LANES, LANES)
                s_re = data[0, krows, cols].astype(jnp.float32)
                s_im = data[1, krows, cols].astype(jnp.float32)
                t_re = s_re * w_re + s_im * w_im
                t_im = s_im * w_re - s_re * w_im
                f_sum = fwd_sum[rows, above]
                f_im = fwd_im[rows, above]
                b_re = bwd_re[rows, below]
                b_sum = bwd_sum[rows, below]
                b_dif = bwd_dif[rows, below]
                shared = b_re * f_sum
                p_re = shared - f_im * b_dif
                p_im = shared - fwd_re[rows, above] * b_sum
                r_re = t_re - mag * p_re
                r_im = t_im - mag * p_im
                e_sum = e_sum + (r_re * r_re + r_im * r_im)
                a_re = a_re + (r_re * p_re + r_im * p_im)
                a_im = a_im + (r_im * p_re - r_re * p_im)
                x_re = mag * r_re
                x_im = mag * r_im
                x_sum = x_re + x_im
                shared = b_re * x_sum
                u_re = shared - x_im * b_sum
                u_im = shared - x_re * b_dif
                shared = f_im * x_sum
                d_re = shared + x_re * fwd_dif[rows, above]
                d_im = shared - x_im * f_sum
                if q == 0:
                    up_re[rows, above] = u_re
                    up_im[rows, above] = u_im
                    down_re[rows, below] = d_re
                    down_im[rows, below] = d_im
                else:
                    up_re[rows, above] += u_re
                    up_im[rows, above] += u_im
                    down_re[rows, below] += d_re
                    down_im[rows, below] += d_im
            part_re[krows, :] = a_re
            part_im[krows, :] = a_im
            err[...] = e_sum
            return carry

        lax.fori_loop(0, ROWS // GROUP, group, 0, unroll=UNROLL)

    ones = jnp.ones((8, LANES), jnp.float32)
    pieces = 4
    span = (owned + halo) // pieces
    raised = [[], []]
    lowered = [[], []]
    for piece in range(pieces):
        high = slice(halo - LANES + piece * span, halo + piece * span + span)
        low = slice(piece * span, piece * span + span + LANES)
        totals = [jnp.zeros((8, span + LANES), jnp.float32)] * 4
        for a in range(ROWS // 8):
            rows = slice(8 * a, 8 * a + 8)
            back = span + LANES - 8 * a
            totals[0] = totals[0] + pltpu.roll(up_re[rows, high], 8 * a, 1, stride=1, stride_axis=0)
            totals[1] = totals[1] + pltpu.roll(up_im[rows, high], 8 * a, 1, stride=1, stride_axis=0)
            totals[2] = totals[2] + (pltpu.roll(down_re[rows, low], back, 1) if a else down_re[rows, low])
            totals[3] = totals[3] + (pltpu.roll(down_im[rows, low], back, 1) if a else down_im[rows, low])
        for part in range(2):
            raised[part].append(totals[part][:, LANES:])
            lowered[part].append(totals[2 + part])
    raised = jnp.concatenate(raised[0] + raised[1], axis=0)
    lowered = skew(jnp.concatenate(lowered[0] + lowered[1], axis=0), -1)[:, :span]
    raised = factor * jnp.sum(raised.reshape(2 * pieces, 8, span), axis=1)
    lowered = factor * jnp.sum(lowered.reshape(2 * pieces, 8, span), axis=1)
    for part in range(2):
        row = slice(part, part + 1)
        rise = jnp.concatenate([raised[pieces * part + i : pieces * part + i + 1] for i in range(pieces)], axis=1)
        fall = jnp.concatenate([lowered[pieces * part + i : pieces * part + i + 1] for i in range(pieces)], axis=1)
        out[row, 0:halo] = fall[:, :halo] * keep_low
        out[row, halo : halo + owned] = fall[:, halo:] + rise[:, :owned]
        out[row, halo + owned : width] = rise[:, owned:] * keep_high
    turned = []
    for sums in (part_re, part_im):
        rest = sums[...]
        line = jnp.zeros((8, harmonics), jnp.float32)
        for _ in range(3):
            term = rest.astype(jnp.bfloat16)
            rest = rest - term.astype(jnp.float32)
            line = line + lax.dot_general(
                ones.astype(jnp.bfloat16),
                term,
                (((1,), (1,)), ((), ())),
                preferred_element_type=jnp.float32,
            )
        turned.append(line[0:1, :])
    line = turned[0] * turn_re - turned[1] * turn_im
    out[0:1, width : width + harmonics] = factor * line
    line = turned[0] * turn_im + turned[1] * turn_re
    out[1:2, width : width + harmonics] = factor * line
    out[0:1, width + harmonics :] = jnp.sum(err[...], axis=0, keepdims=True)
    out[1:2, width + harmonics :] = jnp.zeros((1, LANES), jnp.float32)


def local_gradients(factor, spectra, own, prof, prev, after):
    harmonics = prof.shape[1]
    owned = own.shape[1]
    width = owned + 2 * harmonics
    table = pltpu.VMEM((ROWS, width), jnp.float32)
    column = pltpu.VMEM((harmonics, LANES), jnp.float32)
    anywhere = pl.BlockSpec(memory_space=pltpu.HBM)
    inside = pl.BlockSpec(memory_space=pltpu.VMEM)
    return pl.pallas_call(
        functools.partial(gradient_kernel, factor),
        in_specs=[anywhere, inside, inside, inside, inside],
        out_specs=inside,
        out_shape=jax.ShapeDtypeStruct((2, width + harmonics + LANES), jnp.float32),
        scratch_shapes=[
            pltpu.VMEM((2, harmonics, owned), jnp.bfloat16),
        ]
        + [table] * 11
        + [column] * 5
        + [
            pltpu.VMEM((GROUP, LANES), jnp.float32),
            pltpu.SemaphoreType.DMA((harmonics // ROWS,)),
        ],
        compiler_params=pltpu.CompilerParams(vmem_limit_bytes=VMEM_LIMIT),
    )(pltpu.with_memory_space_constraint(spectra, pltpu.HBM), prof, own, prev, after)


def final_kernel(weight, sums, grads, low_add, high_add, filt, prof, filt_out, prof_out, misfit):
    harmonics = prof.shape[1]
    owned = filt.shape[1]
    halo = harmonics
    squares = jnp.sum(sums[:, harmonics + LANES :])
    scale = filter_rate / jnp.sqrt(jnp.full((2, LANES), squares) / (2 * CHANNELS) + epsilon)
    scale = scale[:, 0:1]
    low = grads[:, halo : 2 * halo] + low_add[:, halo:]
    middle = grads[:, 2 * halo : owned]
    high = grads[:, owned : owned + halo] + high_add[:, :halo]
    filt_out[:, :halo] = filt[:, :halo] - scale * low
    filt_out[:, halo : owned - halo] = filt[:, halo : owned - halo] - scale * middle
    filt_out[:, owned - halo :] = filt[:, owned - halo :] - scale * high
    grad = sums[:, :harmonics]
    mean = jnp.sum(grad * grad) / (2 * harmonics)
    rate = profile_rate / jnp.sqrt(jnp.full((2, LANES), mean) + epsilon)
    prof_out[...] = prof[...] - rate[:, 0:1] * grad
    total = jnp.sum(sums[:, harmonics : harmonics + LANES])
    misfit[0] = total * (weight / CHANNELS)


def update(weight, sums, grads, low_add, high_add, filt, prof):
    inside = pl.BlockSpec(memory_space=pltpu.VMEM)
    return pl.pallas_call(
        functools.partial(final_kernel, weight),
        in_specs=[inside] * 6,
        out_specs=[inside, inside, pl.BlockSpec(memory_space=pltpu.SMEM)],
        out_shape=[
            jax.ShapeDtypeStruct(filt.shape, jnp.float32),
            jax.ShapeDtypeStruct(prof.shape, jnp.float32),
            jax.ShapeDtypeStruct((1,), jnp.float32),
        ],
        compiler_params=pltpu.CompilerParams(vmem_limit_bytes=2 * 1024 * 1024),
    )(sums, grads, low_add, high_add, filt, prof)


def fold(values):
    total = values[:, :LANES]
    for start in range(LANES, values.shape[1], LANES):
        total = total + values[:, start : start + LANES]
    return total


def swap(values, axis, mask):
    count = lax.axis_size(axis)
    return lax.ppermute(values, axis, [(i, i ^ mask) for i in range(count)])


def neighbours(to_next, to_previous, axis):
    count = lax.axis_size(axis)
    ahead = [(i, (i + 1) % count) for i in range(count)]
    back = [(target, source) for source, target in ahead]
    return lax.ppermute(to_next, axis, ahead), lax.ppermute(to_previous, axis, back)


def join_blocks(sums, low_edge, high_edge, axis, masks):
    chan = lax.axis_index(axis)
    size = sums.shape[1]
    span = low_edge.shape[1]
    low_add = jnp.zeros_like(low_edge)
    high_add = jnp.zeros_like(high_edge)
    for step, mask in enumerate(masks):
        is_low = (chan >> step) & 1 == 0
        place = chan & ((1 << step) - 1)
        if step < len(masks) - 1:
            got = swap(jnp.concatenate([sums, low_edge, high_edge], axis=1), axis, mask)
            facing = jnp.where(is_low, got[:, size : size + span], got[:, size + span :])
        else:
            got = swap(jnp.concatenate([sums, jnp.where(is_low, high_edge, low_edge)], axis=1), axis, mask)
            facing = got[:, size:]
        mine = jnp.where(is_low, high_edge, low_edge)
        cross = 2.0 * fold(mine * facing)
        sums = sums + got[:, :size]
        sums = jnp.concatenate([sums[:, : size - LANES], sums[:, size - LANES :] + cross], axis=1)
        high_add = jnp.where(is_low & (place == (1 << step) - 1), facing, high_add)
        low_add = jnp.where(~is_low & (place == 0), facing, low_add)
        if step < len(masks) - 1:
            low_edge = jnp.where(is_low, low_edge, got[:, size : size + span])
            high_edge = jnp.where(is_low, got[:, size + span :], high_edge)
    return sums, low_add, high_add


def on_device(spectra, filter_init, profile_init):
    harmonics = profile_init.shape[1]
    owned = filter_init.shape[1]
    width = owned + 2 * harmonics
    weight = 1.0 / (lax.axis_size("sub") * spectra.shape[0] * harmonics)
    prev, after = neighbours(filter_init, filter_init, "chan")
    scale = jnp.where(lax.axis_index("chan") >= 0, 1.0, 0.0).astype(jnp.float32)
    own = filter_init * scale
    local = local_gradients(-2.0 * weight, spectra, own, profile_init * scale, prev, after)
    for mask in (2, 6, 1):
        local = local + swap(local, "sub", mask)
    grads = local[:, :width]
    sums = jnp.concatenate([local[:, width:], fold(grads * grads)], axis=1)
    sums, low_add, high_add = join_blocks(
        sums, grads[:, : 2 * harmonics], grads[:, owned:], "chan", (1, 2, 4, 12)
    )
    return tuple(update(weight, sums, grads, low_add, high_add, filter_init, profile_init))


def solution(mesh):
    return jax.shard_map(
        on_device,
        mesh=mesh,
        in_specs=(P("sub", None, None, "chan"), P(None, "chan"), P()),
        out_specs=(P(None, "chan"), P(), P()),
        check_vma=False,
    )
```
